32 devices in a mesh: row: 8 (over y, x, core), col: 4 (over z).
Axes of the slice: x: 2, y: 2, z: 4, core: 2. Of those that a mesh axis runs over, the one named last changes fastest.
Arguments:
- covariance: float32 [2048, 2048], P('row', 'col'), may hold values from -5 to 60, as said below
- dynamics: float32 [16, 5, 128, 128], P('row', None, 'col'), may hold values from -0.25 to 0.25
- noise_factor: float32 [16, 128, 128], P('row', 'col'), may hold values from -4 to 4
Outputs:
- forecast: float32 [2048, 2048], P('row', 'col')
The draws below stay inside these ranges and needn't reach their ends.
Inputs may be any that keep to these rules, and one draw needn't show every extreme that they name: covariance is symmetric.
All inputs are finite; a program needn't handle non-finite values.
Results may differ from the reference program's by a relative error of at most 0.00012.
Values sent between devices are 32-bit elements; how exact they have to be, the bound alone decides.
A program may use at most 64 MiB of HBM per device.

```python
import jax
import jax.numpy as jnp
from jax import lax

B = 128
STEPS = 2
N = 2048
NB = 16


def draw_covariance(key, part):
    key_raw, key_diag = jax.random.split(jax.random.fold_in(key, 11), 2)
    raw = jax.random.normal(key_raw, (N, N), jnp.float32)
    sym = 0.5 * (raw + raw.T) * 0.05
    diag = jax.random.uniform(key_diag, (N,), jnp.float32, 2.0, 8.0)
    where = jnp.arange(N, dtype=jnp.int32)
    return sym.at[where, where].add(diag)


def block_scale(own_key, extent, pieces, low, largest):
    factor_of = 1.0
    for position, shards_of in pieces:
        heights = jax.random.uniform(jax.random.fold_in(jax.random.fold_in(own_key, 6), position), (shards_of,), jnp.float32, low / len(pieces), largest / len(pieces))
        factor_of = factor_of * jnp.repeat(jnp.exp(heights), extent[position] // shards_of).reshape((-1,) + (1,) * (len(extent) - 1 - position))
    return factor_of


def normal_values(own_key, dims, width, limit, shards=(), kind=jnp.bfloat16):
    loudness = block_scale(own_key, dims, shards, -0.22, 0.18) if shards else 1.0
    drawn = jax.random.normal(own_key, dims, jnp.float32) * width * loudness
    return jnp.minimum(jnp.maximum(drawn, -limit), limit).astype(kind)


def setup_inputs(seed: int = 0) -> dict:
    seeds = jax.random.split(jax.random.key(seed), 4)
    return {
        "covariance": draw_covariance(jax.random.fold_in(seeds[3], 71), 0),
        "dynamics": normal_values(seeds[1], (NB, 5, B, B), (5 * B) ** -0.5, 0.25, ((0, 8), (2, 4)), jnp.float32),
        "noise_factor": normal_values(seeds[2], (NB, B, B), 0.3, 4.0, ((0, 8), (1, 4)), jnp.float32),
    }


def band_rows(dynamics, matrix):
    padded = jnp.pad(matrix, ((2 * B, 2 * B), (0, 0)))

    def one_band(index):
        window = lax.dynamic_slice_in_dim(padded, index * B, 5 * B, 0).reshape(5, B, matrix.shape[1])
        return jnp.einsum('oab,obn->an', dynamics[index], window, precision=lax.Precision.HIGHEST)

    out = lax.map(one_band, jnp.arange(NB, dtype=jnp.int32))
    return out.reshape(NB * B, matrix.shape[1])


def reference(covariance, dynamics, noise_factor):
    noise = 0.5 * (noise_factor + jnp.swapaxes(noise_factor, 1, 2))
    index = jnp.arange(NB, dtype=jnp.int32)
    state = covariance
    for step in range(STEPS):
        first = band_rows(dynamics, state)
        second = band_rows(dynamics, first.T).T
        blocks = second.reshape(NB, B, NB, B)
        blocks = blocks.at[index, :, index, :].add(noise)
        state = blocks.reshape(N, N)
    return state
```

```python
import functools

import jax
import jax.numpy as jnp
from jax import lax
from jax.experimental import pallas as pl
from jax.experimental.pallas import tpu as pltpu
from jax.sharding import PartitionSpec as P

STEPS = 2
MESH = pl.DeviceIdType.MESH
F32 = jnp.float32
BF16 = jnp.bfloat16


def split(value):
    hi = value.astype(BF16)
    return hi, (value - hi.astype(F32)).astype(BF16)


def product(a, b, transposed):
    dims = (((1,), (1,)), ((), ())) if transposed else (((1,), (0,)), ((), ()))
    dot = functools.partial(lax.dot_general, dimension_numbers=dims, preferred_element_type=F32)
    return dot(a[0], b[0]) + (dot(a[0], b[1]) + dot(a[1], b[0]))


def swap_pairs(i):
    return i + ((i // 2) % 2) * (1 - 2 * (i % 2))


def kernel(
    n_rows, n_cols, cov, dyn, fac, out,
    pe, xe, drow, dcol, nbuf, arow, acol, noise, obuf,
    local_sem, out_sem, zu_s, zu_r, zd_s, zd_r, rg_s, rg_r, sb_s, sb_r, nz_s, nz_r,
    pu_s, pu_r, pd_s, pd_r, xl_s, xl_r, xr_s, xr_r,
):
    rows, cols = cov.shape
    band = rows // 2
    half = cols // 2
    r = lax.axis_index("row")
    c = lax.axis_index("col")
    k, q = r % 2, r // 2
    n_chips = n_rows // 2
    here = swap_pairs(q)
    home = swap_pairs(c)
    distance = (here - home + n_chips) % n_chips
    step_on = 1 - 2 * k
    ring_to = swap_pairs((here + step_on + n_chips) % n_chips) * 2 + k
    ahead = jnp.where(k == 0, distance, (n_chips - distance) % n_chips)
    is_home = q == c
    sibling = r + 1 - 2 * k
    up = (r + n_rows - 1) % n_rows
    down = (r + 1) % n_rows
    left = (c + n_cols - 1) % n_cols
    right = (c + 1) % n_cols
    pending = []

    def put(cond, src, dst, send_sem, recv_sem, to):
        def make():
            return pltpu.make_async_remote_copy(
                src_ref=src, dst_ref=dst, send_sem=send_sem, recv_sem=recv_sem,
                device_id=to, device_id_type=MESH)

        @pl.when(cond)
        def _():
            make().start()

        pending.append((cond, make))

    def arrive(cond, dst, send_sem, recv_sem):
        @pl.when(cond)
        def _():
            pltpu.make_async_remote_copy(
                src_ref=dst, dst_ref=dst, send_sem=send_sem, recv_sem=recv_sem,
                device_id=(sibling, c), device_id_type=MESH).wait_recv()

    own = [pltpu.make_async_copy(cov.at[:, pl.ds(h * half, half)], pe.at[0, h, 1], local_sem.at[h]) for h in range(2)]
    own_dyn = pltpu.make_async_copy(dyn, drow.at[c], local_sem.at[2])
    own_fac = pltpu.make_async_copy(fac, nbuf.at[c], local_sem.at[3])
    for copy in (own_dyn, own_fac, own[0], own[1]):
        copy.start()

    barrier = pltpu.get_barrier_semaphore()
    for i in range(1, n_rows):
        pl.semaphore_signal(barrier, inc=1, device_id=((r + i) % n_rows, c), device_id_type=MESH)
    for i in range(1, n_cols):
        pl.semaphore_signal(barrier, inc=1, device_id=(r, (c + i) % n_cols), device_id_type=MESH)
    pl.semaphore_wait(barrier, n_rows + n_cols - 2)

    not_first, not_last = r > 0, r < n_rows - 1
    has_left, has_right = c > 0, c < n_cols - 1

    def send_half(step, h):
        src = cov.at[:, pl.ds(h * half, half)] if step == 0 else pe.at[step, h, 1]
        put(not_last, src, pe.at[step, h, 0], pd_s.at[step, h], pd_r.at[step, h], (down, c))
        put(not_first, src, pe.at[step, h, 2], pu_s.at[step, h], pu_r.at[step, h], (up, c))

    def to_plane(shard, src):
        put(is_home, src, dcol.at[k, shard], rg_s.at[shard], rg_r.at[shard], (ring_to, c))
        put(is_home, src, dcol.at[k, shard], sb_s.at[0, shard], sb_r.at[k, shard], (sibling, c))

    def ring_relay(cond, shard):
        cond = jnp.logical_and(cond, jnp.logical_not(is_home))
        block = dcol.at[k, shard]
        arrive(cond, block, rg_s.at[shard], rg_r.at[shard])
        put(jnp.logical_and(cond, ahead < n_chips - 1), block, block, rg_s.at[shard], rg_r.at[shard], (ring_to, c))
        put(cond, block, block, sb_s.at[1, shard], sb_r.at[k, shard], (sibling, c))

    put(has_right, dyn, drow.at[c], zu_s.at[c], zu_r.at[c], (r, right))
    put(has_left, dyn, drow.at[c], zd_s.at[c], zd_r.at[c], (r, left))
    to_plane(c, dyn)
    put(jnp.logical_not(is_home), fac, nbuf.at[c], nz_s, nz_r.at[c], (r, q))
    send_half(0, 0)
    send_half(0, 1)

    for step in range(STEPS):
        @pl.when(jnp.logical_not(not_first))
        def _():
            for h in range(2):
                pe[step, h, 0] = jnp.zeros((rows, half), F32)

        @pl.when(jnp.logical_not(not_last))
        def _():
            for h in range(2):
                pe[step, h, 2] = jnp.zeros((rows, half), F32)

        @pl.when(jnp.logical_not(has_left))
        def _():
            xe[step, 0] = jnp.zeros((rows, half), F32)

        @pl.when(jnp.logical_not(has_right))
        def _():
            xe[step, 3] = jnp.zeros((rows, half), F32)

    zero = jnp.zeros((band, band), BF16)
    for part in range(2):
        arow[part, 0, band:, :band] = zero
        arow[part, 2, :band, band:] = zero
        for j in range(2):
            acol[j, part, 0, band:, :band] = zero
            acol[j, part, 2, :band, band:] = zero
    noise[...] = jnp.zeros_like(noise)

    def column_hop(s):
        shard_up = jnp.maximum(c - s, 0)
        shard_down = jnp.minimum(c + s, n_cols - 1)
        from_left, from_right = c - s >= 0, c + s < n_cols
        block = drow.at[shard_up]
        arrive(from_left, block, zu_s.at[shard_up], zu_r.at[shard_up])
        put(jnp.logical_and(from_left, has_right), block, block, zu_s.at[shard_up], zu_r.at[shard_up], (r, right))
        other = drow.at[shard_down]
        arrive(from_right, other, zd_s.at[shard_down], zd_r.at[shard_down])
        put(jnp.logical_and(from_right, has_left), other, other, zd_s.at[shard_down], zd_r.at[shard_down], (r, left))
        for cond, shard in ((from_left, shard_up), (from_right, shard_down)):
            go = jnp.logical_and(cond, is_home)
            src = drow.at[shard]
            put(go, src, dcol.at[k, shard], rg_s.at[shard], rg_r.at[shard], (ring_to, c))
            put(go, src, dcol.at[k, shard], sb_s.at[0, shard], sb_r.at[k, shard], (sibling, c))

    def plane_hop(s):
        if s == 0:
            ring_relay(r >= 0, c)
        else:
            ring_relay(c - s >= 0, jnp.maximum(c - s, 0))
            ring_relay(c + s < n_cols, jnp.minimum(c + s, n_cols - 1))

    for s in range(1, n_cols):
        column_hop(s)
        plane_hop(s - 1)
    own_dyn.wait()

    def assemble(source, target):
        def block(i, o):
            return source[:, i, o].reshape(band, band)

        for i in range(2):
            for o in range(5):
                at = i + o
                hi, lo = split(block(i, o))
                span = pl.ds((at % 2) * band, band)
                target[0, at // 2, i * band:(i + 1) * band, span] = hi
                target[1, at // 2, i * band:(i + 1) * band, span] = lo

    assemble(drow, arow)
    own[0].wait()
    own[1].wait()

    def first_half(step, h):
        total = product((arow[0, 1], arow[1, 1]), split(pe[step, h, 1]), False)
        arrive(not_first, pe.at[step, h, 0], pd_s.at[step, h], pd_r.at[step, h])
        total += product((arow[0, 0], arow[1, 0]), split(pe[step, h, 0]), False)
        arrive(not_last, pe.at[step, h, 2], pu_s.at[step, h], pu_r.at[step, h])
        total += product((arow[0, 2], arow[1, 2]), split(pe[step, h, 2]), False)
        xe[step, 1 + h] = total
        if h == 0:
            put(has_left, xe.at[step, 1], xe.at[step, 3], xl_s.at[step], xl_r.at[step], (r, left))
        else:
            put(has_right, xe.at[step, 2], xe.at[step, 0], xr_s.at[step], xr_r.at[step], (r, right))

    def second_half(step, h):
        def term(t):
            return product(split(xe[step, h + t]), (acol[h, 0, t], acol[h, 1, t]), True)

        if h == 0:
            total = term(1) + term(2) + noise[0]
            arrive(has_left, xe.at[step, 0], xr_s.at[step], xr_r.at[step])
            total += term(0)
        else:
            total = term(0) + term(1) + noise[1]
            arrive(has_right, xe.at[step, 3], xl_s.at[step], xl_r.at[step])
            total += term(2)
        if step + 1 < STEPS:
            pe[step + 1, h, 1] = total
            send_half(step + 1, h)
        else:
            obuf[h] = total
            pltpu.make_async_copy(obuf.at[h], out.at[:, pl.ds(h * half, half)], out_sem.at[h]).start()

    for h in range(2):
        first_half(0, h)

    own_fac.wait()
    for z in range(n_cols):
        arrive(jnp.logical_and(is_home, c != z), nbuf.at[z], nz_s, nz_r.at[z])

    @pl.when(is_home)
    def _():
        for i in range(2):
            block = nbuf[:, i].reshape(band, band)
            block = 0.5 * (block + block.T)
            noise[k, i * band:(i + 1) * band, i * band:(i + 1) * band] = block

    plane_hop(n_cols - 1)

    @pl.when(is_home)
    def _():
        acol[k] = arow[...]

    @pl.when(jnp.logical_not(is_home))
    def _():
        assemble(dcol.at[k], acol.at[k])

    for z in range(n_cols):
        arrive(r >= 0, dcol.at[1 - k, z], sb_s.at[0, z], sb_r.at[1 - k, z])
    assemble(dcol.at[1 - k], acol.at[1 - k])

    for step in range(STEPS):
        order = (1, 0) if step % 2 == 0 else (0, 1)
        if step > 0:
            for h in order[::-1]:
                first_half(step, h)
        for h in order:
            second_half(step, h)

    for h in range(2):
        pltpu.make_async_copy(obuf.at[h], out.at[:, pl.ds(h * half, half)], out_sem.at[h]).wait()
    for cond, make in pending:
        @pl.when(cond)
        def _(make=make):
            make().wait_send()


def body(n_rows, n_cols, covariance, dynamics, noise_factor):
    rows, cols = covariance.shape
    band = dynamics.shape[3]
    half = cols // 2
    dma = pltpu.SemaphoreType.DMA
    shards = (n_cols,)
    pairs = (STEPS, 2)
    return pl.pallas_call(
        functools.partial(kernel, n_rows, n_cols),
        out_shape=jax.ShapeDtypeStruct((rows, cols), F32),
        in_specs=[pl.BlockSpec(memory_space=pl.ANY)] * 3,
        out_specs=pl.BlockSpec(memory_space=pl.ANY),
        scratch_shapes=[
            pltpu.VMEM((STEPS, 2, 3, rows, half), F32),
            pltpu.VMEM((STEPS, 4, rows, half), F32),
            pltpu.VMEM((n_cols,) + dynamics.shape, F32),
            pltpu.VMEM((2, n_cols) + dynamics.shape, F32),
            pltpu.VMEM((n_cols,) + noise_factor.shape, F32),
            pltpu.VMEM((2, 3, rows, rows), BF16),
            pltpu.VMEM((2, 2, 3, rows, rows), BF16),
            pltpu.VMEM((2, rows, half), F32),
            pltpu.VMEM((2, rows, half), F32),
            dma((4,)), dma((2,)),
            dma(shards), dma(shards), dma(shards), dma(shards),
            dma(shards), dma(shards), dma((2,) + shards), dma((2,) + shards),
            dma, dma(shards),
            dma(pairs), dma(pairs), dma(pairs), dma(pairs),
            dma((STEPS,)), dma((STEPS,)), dma((STEPS,)), dma((STEPS,)),
        ],
        compiler_params=pltpu.CompilerParams(
            collective_id=0, has_side_effects=True, vmem_limit_bytes=40 * 1024 * 1024),
    )(covariance, dynamics, noise_factor)


def solution(mesh):
    in_specs = (P("row", "col"), P("row", None, "col", None), P("row", "col", None))
    out_specs = P("row", "col")
    run = functools.partial(body, mesh.shape["row"], mesh.shape["col"])
    return jax.shard_map(run, mesh=mesh, in_specs=in_specs, out_specs=out_specs, check_vma=False)
```

```python
import functools

import jax
import jax.numpy as jnp
from jax import lax
from jax.experimental import pallas as pl
from jax.experimental.pallas import tpu as pltpu
from jax.sharding import PartitionSpec as P

STEPS = 2
MESH = pl.DeviceIdType.MESH
F32 = jnp.float32
BF16 = jnp.bfloat16


def split(value):
    hi = value.astype(BF16)
    return hi, (value - hi.astype(F32)).astype(BF16)


def product(a, b, transposed):
    dims = (((1,), (1,)), ((), ())) if transposed else (((1,), (0,)), ((), ()))
    dot = functools.partial(lax.dot_general, dimension_numbers=dims, preferred_element_type=F32)
    return dot(a[0], b[0]) + (dot(a[0], b[1]) + dot(a[1], b[0]))


def swap_pairs(i):
    return i + ((i // 2) % 2) * (1 - 2 * (i % 2))


def kernel(
    n_rows, n_cols, cov, dyn, fac, out,
    pe, xe, drow, dcol, nbuf, arow, acol, noise, obuf,
    local_sem, out_sem, zu_s, zu_r, zd_s, zd_r, rg_s, rg_r, sb_s, sb_r, nz_s, nz_r,
    pu_s, pu_r, pd_s, pd_r, xl_s, xl_r, xr_s, xr_r,
):
    rows, cols = cov.shape
    band = rows // 2
    half = cols // 2
    r = lax.axis_index("row")
    c = lax.axis_index("col")
    k, q = r % 2, r // 2
    n_chips = n_rows // 2
    here = swap_pairs(q)
    home = swap_pairs(c)
    distance = (here - home + n_chips) % n_chips
    step_on = 1 - 2 * k
    ring_to = swap_pairs((here + step_on + n_chips) % n_chips) * 2 + k
    ahead = jnp.where(k == 0, distance, (n_chips - distance) % n_chips)
    is_home = q == c
    sibling = r + 1 - 2 * k
    up = (r + n_rows - 1) % n_rows
    down = (r + 1) % n_rows
    left = (c + n_cols - 1) % n_cols
    right = (c + 1) % n_cols
    pending = []

    def put(cond, src, dst, send_sem, recv_sem, to):
        def make():
            return pltpu.make_async_remote_copy(
                src_ref=src, dst_ref=dst, send_sem=send_sem, recv_sem=recv_sem,
                device_id=to, device_id_type=MESH)

        @pl.when(cond)
        def _():
            make().start()

        pending.append((cond, make))

    def arrive(cond, dst, send_sem, recv_sem):
        @pl.when(cond)
        def _():
            pltpu.make_async_remote_copy(
                src_ref=dst, dst_ref=dst, send_sem=send_sem, recv_sem=recv_sem,
                device_id=(sibling, c), device_id_type=MESH).wait_recv()

    own = [pltpu.make_async_copy(cov.at[:, pl.ds(h * half, half)], pe.at[0, h, 1], local_sem.at[h]) for h in range(2)]
    own_dyn = pltpu.make_async_copy(dyn, drow.at[c], local_sem.at[2])
    own_fac = pltpu.make_async_copy(fac, nbuf.at[c], local_sem.at[3])
    for copy in (own_dyn, own_fac, own[0], own[1]):
        copy.start()

    barrier = pltpu.get_barrier_semaphore()
    for i in range(1, n_rows):
        pl.semaphore_signal(barrier, inc=1, device_id=((r + i) % n_rows, c), device_id_type=MESH)
    for i in range(1, n_cols):
        pl.semaphore_signal(barrier, inc=1, device_id=(r, (c + i) % n_cols), device_id_type=MESH)
    pl.semaphore_wait(barrier, n_rows + n_cols - 2)

    not_first, not_last = r > 0, r < n_rows - 1
    has_left, has_right = c > 0, c < n_cols - 1

    def send_half(step, h):
        src = cov.at[:, pl.ds(h * half, half)] if step == 0 else pe.at[step, h, 1]
        put(not_last, src, pe.at[step, h, 0], pd_s.at[step, h], pd_r.at[step, h], (down, c))
        put(not_first, src, pe.at[step, h, 2], pu_s.at[step, h], pu_r.at[step, h], (up, c))

    def to_plane(cond, z, i, src):
        go = jnp.logical_and(cond, is_home)
        put(go, src, dcol.at[k, z, i], rg_s.at[z, i], rg_r.at[z, i], (ring_to, c))
        put(go, src, dcol.at[k, z, i], sb_s.at[0, z, i], sb_r.at[k, z, i], (sibling, c))

    def ring_relay(cond, z, i, passes):
        block = dcol.at[k, z, i]
        arrive(cond, block, rg_s.at[z, i], rg_r.at[z, i])
        if passes:
            put(cond, block, block, rg_s.at[z, i], rg_r.at[z, i], (ring_to, c))
        put(cond, block, block, sb_s.at[1, z, i], sb_r.at[k, z, i], (sibling, c))

    for i in range(2):
        put(has_right, dyn.at[i], drow.at[c, i], zu_s.at[c, i], zu_r.at[c, i], (r, right))
        put(has_left, dyn.at[i], drow.at[c, i], zd_s.at[c, i], zd_r.at[c, i], (r, left))
    for i in range(2):
        to_plane(r >= 0, c, i, dyn.at[i])
    put(jnp.logical_not(is_home), fac, nbuf.at[c], nz_s, nz_r.at[c], (r, q))
    send_half(0, 0)
    send_half(0, 1)

    for step in range(STEPS):
        @pl.when(jnp.logical_not(not_first))
        def _():
            for h in range(2):
                pe[step, h, 0] = jnp.zeros((rows, half), F32)

        @pl.when(jnp.logical_not(not_last))
        def _():
            for h in range(2):
                pe[step, h, 2] = jnp.zeros((rows, half), F32)

        @pl.when(jnp.logical_not(has_left))
        def _():
            xe[step, 0] = jnp.zeros((rows, half), F32)

        @pl.when(jnp.logical_not(has_right))
        def _():
            xe[step, 3] = jnp.zeros((rows, half), F32)

    zero = jnp.zeros((band, band), BF16)
    for part in range(2):
        arow[part, 0, band:, :band] = zero
        arow[part, 2, :band, band:] = zero
        for j in range(2):
            acol[j, part, 0, band:, :band] = zero
            acol[j, part, 2, :band, band:] = zero
    noise[...] = jnp.zeros_like(noise)

    def sources(s):
        found = [(c - s >= 0, jnp.maximum(c - s, 0))]
        return found if s == 0 else found + [(c + s < n_cols, jnp.minimum(c + s, n_cols - 1))]

    def column_hop(s, i):
        (from_left, low), (from_right, high) = sources(s)
        block = drow.at[low, i]
        arrive(from_left, block, zu_s.at[low, i], zu_r.at[low, i])
        put(jnp.logical_and(from_left, has_right), block, block, zu_s.at[low, i], zu_r.at[low, i], (r, right))
        other = drow.at[high, i]
        arrive(from_right, other, zd_s.at[high, i], zd_r.at[high, i])
        put(jnp.logical_and(from_right, has_left), other, other, zd_s.at[high, i], zd_r.at[high, i], (r, left))
        to_plane(from_left, low, i, block)
        to_plane(from_right, high, i, other)

    def plane_hop(event, who, passes=True):
        for cond, z in sources(event // 2):
            ring_relay(jnp.logical_and(cond, who), z, event % 2, passes)

    n_events = 2 * n_cols
    leaf = ahead == n_chips - 1
    near = jnp.logical_and(ahead == 1, jnp.logical_not(leaf))
    far = jnp.logical_and(ahead > 1, jnp.logical_not(leaf))
    near_lag, far_lag = 2, 4
    for event in range(2, n_events):
        column_hop(event // 2, event % 2)
        if event >= near_lag:
            plane_hop(event - near_lag, near)
        if event >= far_lag:
            plane_hop(event - far_lag, far)
    own_dyn.wait()

    def assemble(source, target):
        def block(i, o):
            return source[:, i, o].reshape(band, band)

        for i in range(2):
            for o in range(5):
                at = i + o
                hi, lo = split(block(i, o))
                span = pl.ds((at % 2) * band, band)
                target[0, at // 2, i * band:(i + 1) * band, span] = hi
                target[1, at // 2, i * band:(i + 1) * band, span] = lo

    assemble(drow, arow)
    own[0].wait()
    own[1].wait()

    def first_half(step, h):
        total = product((arow[0, 1], arow[1, 1]), split(pe[step, h, 1]), False)
        arrive(not_first, pe.at[step, h, 0], pd_s.at[step, h], pd_r.at[step, h])
        total += product((arow[0, 0], arow[1, 0]), split(pe[step, h, 0]), False)
        arrive(not_last, pe.at[step, h, 2], pu_s.at[step, h], pu_r.at[step, h])
        total += product((arow[0, 2], arow[1, 2]), split(pe[step, h, 2]), False)
        xe[step, 1 + h] = total
        if h == 0:
            put(has_left, xe.at[step, 1], xe.at[step, 3], xl_s.at[step], xl_r.at[step], (r, left))
        else:
            put(has_right, xe.at[step, 2], xe.at[step, 0], xr_s.at[step], xr_r.at[step], (r, right))

    def second_half(step, h):
        def term(t):
            return product(split(xe[step, h + t]), (acol[h, 0, t], acol[h, 1, t]), True)

        if h == 0:
            total = term(1) + term(2) + noise[0]
            arrive(has_left, xe.at[step, 0], xr_s.at[step], xr_r.at[step])
            total += term(0)
        else:
            total = term(0) + term(1) + noise[1]
            arrive(has_right, xe.at[step, 3], xl_s.at[step], xl_r.at[step])
            total += term(2)
        if step + 1 < STEPS:
            pe[step + 1, h, 1] = total
            send_half(step + 1, h)
        else:
            obuf[h] = total
            pltpu.make_async_copy(obuf.at[h], out.at[:, pl.ds(h * half, half)], out_sem.at[h]).start()

    for event in range(n_events - near_lag, n_events):
        plane_hop(event, near)
    first_half(0, 0)
    for event in range(n_events - far_lag, n_events):
        plane_hop(event, far)
    first_half(0, 1)

    own_fac.wait()
    for z in range(n_cols):
        arrive(jnp.logical_and(is_home, c != z), nbuf.at[z], nz_s, nz_r.at[z])

    @pl.when(is_home)
    def _():
        for i in range(2):
            block = nbuf[:, i].reshape(band, band)
            block = 0.5 * (block + block.T)
            noise[k, i * band:(i + 1) * band, i * band:(i + 1) * band] = block

    for event in range(n_events):
        plane_hop(event, leaf, False)

    @pl.when(is_home)
    def _():
        acol[k] = arow[...]

    @pl.when(jnp.logical_not(is_home))
    def _():
        assemble(dcol.at[k], acol.at[k])

    for z in range(n_cols):
        for i in range(2):
            arrive(r >= 0, dcol.at[1 - k, z, i], sb_s.at[0, z, i], sb_r.at[1 - k, z, i])
    assemble(dcol.at[1 - k], acol.at[1 - k])

    for step in range(STEPS):
        order = (1, 0) if step % 2 == 0 else (0, 1)
        if step > 0:
            for h in order[::-1]:
                first_half(step, h)
        for h in order:
            second_half(step, h)

    for h in range(2):
        pltpu.make_async_copy(obuf.at[h], out.at[:, pl.ds(h * half, half)], out_sem.at[h]).wait()
    for cond, make in pending:
        @pl.when(cond)
        def _(make=make):
            make().wait_send()


def body(n_rows, n_cols, covariance, dynamics, noise_factor):
    rows, cols = covariance.shape
    band = dynamics.shape[3]
    half = cols // 2
    dma = pltpu.SemaphoreType.DMA
    shards = (n_cols, 2)
    pairs = (STEPS, 2)
    return pl.pallas_call(
        functools.partial(kernel, n_rows, n_cols),
        out_shape=jax.ShapeDtypeStruct((rows, cols), F32),
        in_specs=[pl.BlockSpec(memory_space=pltpu.HBM)] * 3,
        out_specs=pl.BlockSpec(memory_space=pltpu.HBM),
        scratch_shapes=[
            pltpu.VMEM((STEPS, 2, 3, rows, half), F32),
            pltpu.VMEM((STEPS, 4, rows, half), F32),
            pltpu.VMEM((n_cols,) + dynamics.shape, F32),
            pltpu.VMEM((2, n_cols) + dynamics.shape, F32),
            pltpu.VMEM((n_cols,) + noise_factor.shape, F32),
            pltpu.VMEM((2, 3, rows, rows), BF16),
            pltpu.VMEM((2, 2, 3, rows, rows), BF16),
            pltpu.VMEM((2, rows, half), F32),
            pltpu.VMEM((2, rows, half), F32),
            dma((4,)), dma((2,)),
            dma(shards), dma(shards), dma(shards), dma(shards),
            dma(shards), dma(shards), dma((2,) + shards), dma((2,) + shards),
            dma, dma((n_cols,)),
            dma(pairs), dma(pairs), dma(pairs), dma(pairs),
            dma((STEPS,)), dma((STEPS,)), dma((STEPS,)), dma((STEPS,)),
        ],
        compiler_params=pltpu.CompilerParams(
            collective_id=0, has_side_effects=True, vmem_limit_bytes=62 * 1024 * 1024),
    )(covariance, dynamics, noise_factor)


def solution(mesh):
    in_specs = (P("row", "col"), P("row", None, "col", None), P("row", "col", None))
    out_specs = P("row", "col")
    run = functools.partial(body, mesh.shape["row"], mesh.shape["col"])
    return jax.shard_map(run, mesh=mesh, in_specs=in_specs, out_specs=out_specs, check_vma=False)
```

```python
import functools

import jax
import jax.numpy as jnp
from jax import lax
from jax.experimental import pallas as pl
from jax.experimental.pallas import tpu as pltpu
from jax.sharding import PartitionSpec as P

STEPS = 2
MESH = pl.DeviceIdType.MESH
F32 = jnp.float32
BF16 = jnp.bfloat16


def split(value):
    hi = value.astype(BF16)
    return hi, (value - hi.astype(F32)).astype(BF16)


def product(a, b, transposed):
    dims = (((1,), (1,)), ((), ())) if transposed else (((1,), (0,)), ((), ()))
    dot = functools.partial(lax.dot_general, dimension_numbers=dims, preferred_element_type=F32)
    return dot(a[0], b[0]) + (dot(a[0], b[1]) + dot(a[1], b[0]))


def swap_pairs(i):
    return i + ((i // 2) % 2) * (1 - 2 * (i % 2))


def kernel(
    n_rows, n_cols, cov, dyn, fac, out,
    pe, xe, drow, dcol, nbuf, arow, acol, noise, obuf, rbuf,
    local_sem, out_sem, zu_s, zu_r, zd_s, zd_r, rg_s, rg_r, sb_s, sb_r, nz_s, nz_r,
    pu_s, pu_r, pd_s, pd_r, xl_s, xl_r, xr_s, xr_r, rl_s, rl_r,
):
    rows, cols = cov.shape
    band = rows // 2
    half = cols // 2
    r = lax.axis_index("row")
    c = lax.axis_index("col")
    k, q = r % 2, r // 2
    n_chips = n_rows // 2
    here = swap_pairs(q)
    home = swap_pairs(c)
    distance = (here - home + n_chips) % n_chips
    step_on = 1 - 2 * k
    ring_to = swap_pairs((here + step_on + n_chips) % n_chips) * 2 + k
    ahead = jnp.where(k == 0, distance, (n_chips - distance) % n_chips)
    is_home = q == c
    sibling = r + 1 - 2 * k
    up = (r + n_rows - 1) % n_rows
    down = (r + 1) % n_rows
    left = (c + n_cols - 1) % n_cols
    right = (c + 1) % n_cols
    pending = []

    def put(cond, src, dst, send_sem, recv_sem, to):
        def make():
            return pltpu.make_async_remote_copy(
                src_ref=src, dst_ref=dst, send_sem=send_sem, recv_sem=recv_sem,
                device_id=to, device_id_type=MESH)

        @pl.when(cond)
        def _():
            make().start()

        pending.append((cond, make))

    def arrive(cond, dst, send_sem, recv_sem):
        @pl.when(cond)
        def _():
            pltpu.make_async_remote_copy(
                src_ref=dst, dst_ref=dst, send_sem=send_sem, recv_sem=recv_sem,
                device_id=(sibling, c), device_id_type=MESH).wait_recv()

    own = [pltpu.make_async_copy(cov.at[:, pl.ds(h * half, half)], pe.at[0, h, 1], local_sem.at[h]) for h in range(2)]
    own_dyn = pltpu.make_async_copy(dyn, drow.at[c], local_sem.at[2])
    own_fac = pltpu.make_async_copy(fac, nbuf.at[c], local_sem.at[3])
    for copy in (own_dyn, own_fac, own[0], own[1]):
        copy.start()

    barrier = pltpu.get_barrier_semaphore()
    for i in range(1, n_rows):
        pl.semaphore_signal(barrier, inc=1, device_id=((r + i) % n_rows, c), device_id_type=MESH)
    for i in range(1, n_cols):
        pl.semaphore_signal(barrier, inc=1, device_id=(r, (c + i) % n_cols), device_id_type=MESH)
    pl.semaphore_wait(barrier, n_rows + n_cols - 2)

    not_first, not_last = r > 0, r < n_rows - 1
    has_left, has_right = c > 0, c < n_cols - 1

    quarter = half // 2

    def columns(j):
        return pl.ds(j * quarter, quarter)

    detour = n_chips == 4
    upper, lower, last = n_rows // 2 - 1, n_rows // 2, n_rows - 1
    via_down, via_up = last, 0

    def send_half(step, h):
        for j in range(2):
            n = 2 * h + j
            src = cov.at[:, columns(n)] if step == 0 else pe.at[step, h, 1, :, columns(j)]
            goes_down, goes_up = not_last, not_first
            if detour and j == 1:
                goes_down = jnp.logical_and(not_last, r != upper)
                goes_up = jnp.logical_and(not_first, r != lower)
                block = rbuf.at[step, h]
                put(r == upper, src, block, rl_s.at[step, h], rl_r.at[step, h], (via_down, c))
                put(r == lower, src, block, rl_s.at[step, h], rl_r.at[step, h], (via_up, c))
            put(goes_down, src, pe.at[step, h, 0, :, columns(j)], pd_s.at[step, n], pd_r.at[step, n], (down, c))
            put(goes_up, src, pe.at[step, h, 2, :, columns(j)], pu_s.at[step, n], pu_r.at[step, n], (up, c))

    def relay_half(step, h):
        if not detour:
            return
        n, at, block = 2 * h + 1, columns(1), rbuf.at[step, h]
        arrive(jnp.logical_or(r == via_down, r == via_up), block, rl_s.at[step, h], rl_r.at[step, h])
        put(r == via_down, block, pe.at[step, h, 0, :, at], pd_s.at[step, n], pd_r.at[step, n], (lower, c))
        put(r == via_up, block, pe.at[step, h, 2, :, at], pu_s.at[step, n], pu_r.at[step, n], (upper, c))

    def to_plane(cond, z, i, src):
        go = jnp.logical_and(cond, is_home)
        put(go, src, dcol.at[k, z, i], rg_s.at[z, i], rg_r.at[z, i], (ring_to, c))
        put(go, src, dcol.at[k, z, i], sb_s.at[0, z, i], sb_r.at[k, z, i], (sibling, c))

    def ring_relay(cond, z, i, passes):
        block = dcol.at[k, z, i]
        arrive(cond, block, rg_s.at[z, i], rg_r.at[z, i])
        if passes:
            put(cond, block, block, rg_s.at[z, i], rg_r.at[z, i], (ring_to, c))
        put(cond, block, block, sb_s.at[1, z, i], sb_r.at[k, z, i], (sibling, c))

    for i in range(2):
        put(has_right, dyn.at[i], drow.at[c, i], zu_s.at[c, i], zu_r.at[c, i], (r, right))
        put(has_left, dyn.at[i], drow.at[c, i], zd_s.at[c, i], zd_r.at[c, i], (r, left))
    for i in range(2):
        to_plane(r >= 0, c, i, dyn.at[i])
    put(jnp.logical_not(is_home), fac, nbuf.at[c], nz_s, nz_r.at[c], (r, q))
    send_half(0, 0)
    send_half(0, 1)

    for step in range(STEPS):
        @pl.when(jnp.logical_not(not_first))
        def _():
            for h in range(2):
                pe[step, h, 0] = jnp.zeros((rows, half), F32)

        @pl.when(jnp.logical_not(not_last))
        def _():
            for h in range(2):
                pe[step, h, 2] = jnp.zeros((rows, half), F32)

        @pl.when(jnp.logical_not(has_left))
        def _():
            xe[step, 0] = jnp.zeros((rows, half), F32)

        @pl.when(jnp.logical_not(has_right))
        def _():
            xe[step, 3] = jnp.zeros((rows, half), F32)

    zero = jnp.zeros((band, band), BF16)
    for part in range(2):
        arow[part, 0, band:, :band] = zero
        arow[part, 2, :band, band:] = zero
        for j in range(2):
            acol[j, part, 0, band:, :band] = zero
            acol[j, part, 2, :band, band:] = zero
    noise[...] = jnp.zeros_like(noise)

    def sources(s):
        found = [(c - s >= 0, jnp.maximum(c - s, 0))]
        return found if s == 0 else found + [(c + s < n_cols, jnp.minimum(c + s, n_cols - 1))]

    def column_hop(s, i):
        (from_left, low), (from_right, high) = sources(s)
        block = drow.at[low, i]
        arrive(from_left, block, zu_s.at[low, i], zu_r.at[low, i])
        put(jnp.logical_and(from_left, has_right), block, block, zu_s.at[low, i], zu_r.at[low, i], (r, right))
        other = drow.at[high, i]
        arrive(from_right, other, zd_s.at[high, i], zd_r.at[high, i])
        put(jnp.logical_and(from_right, has_left), other, other, zd_s.at[high, i], zd_r.at[high, i], (r, left))
        to_plane(from_left, low, i, block)
        to_plane(from_right, high, i, other)

    def plane_hop(event, who, passes=True):
        for cond, z in sources(event // 2):
            ring_relay(jnp.logical_and(cond, who), z, event % 2, passes)

    n_events = 2 * n_cols
    leaf = ahead == n_chips - 1
    near = jnp.logical_and(ahead == 1, jnp.logical_not(leaf))
    far = jnp.logical_and(ahead > 1, jnp.logical_not(leaf))
    near_lag, far_lag = 5, 8
    for event in range(2, n_events):
        column_hop(event // 2, event % 2)
        if event in (n_events - 3, n_events - 1):
            relay_half(0, (event - n_events + 3) // 2)
        if event >= near_lag:
            plane_hop(event - near_lag, near)
        if event >= far_lag:
            plane_hop(event - far_lag, far)
    own_dyn.wait()

    def assemble(source, target):
        def block(i, o):
            return source[:, i, o].reshape(band, band)

        for i in range(2):
            for o in range(5):
                at = i + o
                hi, lo = split(block(i, o))
                span = pl.ds((at % 2) * band, band)
                target[0, at // 2, i * band:(i + 1) * band, span] = hi
                target[1, at // 2, i * band:(i + 1) * band, span] = lo

    assemble(drow, arow)
    own[0].wait()
    own[1].wait()

    def first_half(step, h):
        inner = product((arow[0, 1], arow[1, 1]), split(pe[step, h, 1]), False)
        for j in range(2):
            n, at = 2 * h + j, columns(j)
            if step > 0 and j == 1:
                relay_half(step, h)
            total = inner[:, j * quarter:(j + 1) * quarter]
            arrive(not_first, pe.at[step, h, 0, :, at], pd_s.at[step, n], pd_r.at[step, n])
            total += product((arow[0, 0], arow[1, 0]), split(pe[step, h, 0, :, at]), False)
            arrive(not_last, pe.at[step, h, 2, :, at], pu_s.at[step, n], pu_r.at[step, n])
            total += product((arow[0, 2], arow[1, 2]), split(pe[step, h, 2, :, at]), False)
            xe[step, 1 + h, :, at] = total
            src = xe.at[step, 1 + h, :, at]
            if h == 0:
                put(has_left, src, xe.at[step, 3, :, at], xl_s.at[step, j], xl_r.at[step, j], (r, left))
            else:
                put(has_right, src, xe.at[step, 0, :, at], xr_s.at[step, j], xr_r.at[step, j], (r, right))

    def second_half(step, h):
        def term(t):
            return product(split(xe[step, h + t]), (acol[h, 0, t], acol[h, 1, t]), True)

        if h == 0:
            total = term(1) + term(2) + noise[0]
            for j in range(2):
                arrive(has_left, xe.at[step, 0, :, columns(j)], xr_s.at[step, j], xr_r.at[step, j])
            total += term(0)
        else:
            total = term(0) + term(1) + noise[1]
            for j in range(2):
                arrive(has_right, xe.at[step, 3, :, columns(j)], xl_s.at[step, j], xl_r.at[step, j])
            total += term(2)
        if step + 1 < STEPS:
            pe[step + 1, h, 1] = total
            send_half(step + 1, h)
        else:
            obuf[h] = total
            pltpu.make_async_copy(obuf.at[h], out.at[:, pl.ds(h * half, half)], out_sem.at[h]).start()

    for event in range(n_events - near_lag, n_events):
        plane_hop(event, near)
    first_half(0, 0)
    for event in range(n_events - far_lag, n_events):
        plane_hop(event, far)
    first_half(0, 1)

    own_fac.wait()
    for z in range(n_cols):
        arrive(jnp.logical_and(is_home, c != z), nbuf.at[z], nz_s, nz_r.at[z])

    @pl.when(is_home)
    def _():
        for i in range(2):
            block = nbuf[:, i].reshape(band, band)
            block = 0.5 * (block + block.T)
            noise[k, i * band:(i + 1) * band, i * band:(i + 1) * band] = block

    for event in range(n_events):
        plane_hop(event, leaf, False)

    @pl.when(is_home)
    def _():
        acol[k] = arow[...]

    @pl.when(jnp.logical_not(is_home))
    def _():
        assemble(dcol.at[k], acol.at[k])

    for z in range(n_cols):
        for i in range(2):
            arrive(r >= 0, dcol.at[1 - k, z, i], sb_s.at[0, z, i], sb_r.at[1 - k, z, i])
    assemble(dcol.at[1 - k], acol.at[1 - k])

    for step in range(STEPS):
        order = (1, 0) if step % 2 == 0 else (0, 1)
        if step > 0:
            for h in order[::-1]:
                first_half(step, h)
        for h in order:
            second_half(step, h)

    for h in range(2):
        pltpu.make_async_copy(obuf.at[h], out.at[:, pl.ds(h * half, half)], out_sem.at[h]).wait()
    for cond, make in pending:
        @pl.when(cond)
        def _(make=make):
            make().wait_send()


def body(n_rows, n_cols, covariance, dynamics, noise_factor):
    rows, cols = covariance.shape
    band = dynamics.shape[3]
    half = cols // 2
    dma = pltpu.SemaphoreType.DMA
    shards = (n_cols, 2)
    pairs = (STEPS, 2)
    quarters = (STEPS, 4)
    return pl.pallas_call(
        functools.partial(kernel, n_rows, n_cols),
        out_shape=jax.ShapeDtypeStruct((rows, cols), F32),
        in_specs=[pl.BlockSpec(memory_space=pltpu.HBM)] * 3,
        out_specs=pl.BlockSpec(memory_space=pltpu.HBM),
        scratch_shapes=[
            pltpu.VMEM((STEPS, 2, 3, rows, half), F32),
            pltpu.VMEM((STEPS, 4, rows, half), F32),
            pltpu.VMEM((n_cols,) + dynamics.shape, F32),
            pltpu.VMEM((2, n_cols) + dynamics.shape, F32),
            pltpu.VMEM((n_cols,) + noise_factor.shape, F32),
            pltpu.VMEM((2, 3, rows, rows), BF16),
            pltpu.VMEM((2, 2, 3, rows, rows), BF16),
            pltpu.VMEM((2, rows, half), F32),
            pltpu.VMEM((2, rows, half), F32),
            pltpu.VMEM((STEPS, 2, rows, half // 2), F32),
            dma((4,)), dma((2,)),
            dma(shards), dma(shards), dma(shards), dma(shards),
            dma(shards), dma(shards), dma((2,) + shards), dma((2,) + shards),
            dma, dma((n_cols,)),
            dma(quarters), dma(quarters), dma(quarters), dma(quarters),
            dma(pairs), dma(pairs), dma(pairs), dma(pairs), dma(pairs), dma(pairs),
        ],
        compiler_params=pltpu.CompilerParams(
            collective_id=0, has_side_effects=True, vmem_limit_bytes=62 * 1024 * 1024),
    )(covariance, dynamics, noise_factor)


def solution(mesh):
    in_specs = (P("row", "col"), P("row", None, "col", None), P("row", "col", None))
    out_specs = P("row", "col")
    run = functools.partial(body, mesh.shape["row"], mesh.shape["col"])
    return jax.shard_map(run, mesh=mesh, in_specs=in_specs, out_specs=out_specs, check_vma=False)
```

```python
import functools

import jax
import jax.numpy as jnp
from jax import lax
from jax.experimental import pallas as pl
from jax.experimental.pallas import tpu as pltpu
from jax.sharding import PartitionSpec as P

STEPS = 2
MESH = pl.DeviceIdType.MESH
F32 = jnp.float32
BF16 = jnp.bfloat16


def split(value):
    hi = value.astype(BF16)
    return hi, (value - hi.astype(F32)).astype(BF16)


def product(a, b, transposed):
    dims = (((1,), (1,)), ((), ())) if transposed else (((1,), (0,)), ((), ()))
    dot = functools.partial(lax.dot_general, dimension_numbers=dims, preferred_element_type=F32)
    return dot(a[0], b[0]) + (dot(a[0], b[1]) + dot(a[1], b[0]))


def swap_pairs(i):
    return i + ((i // 2) % 2) * (1 - 2 * (i % 2))


def kernel(
    n_rows, n_cols, cov, dyn, fac, out,
    pe, xe, drow, dcol, nbuf, arow, acol, noise, obuf, rbuf,
    local_sem, out_sem, zu_s, zu_r, zd_s, zd_r, rg_s, rg_r, sb_s, sb_r, nz_s, nz_r,
    pu_s, pu_r, pd_s, pd_r, xl_s, xl_r, xr_s, xr_r, rl_s, rl_r,
):
    rows, cols = cov.shape
    band = rows // 2
    half = cols // 2
    r = lax.axis_index("row")
    c = lax.axis_index("col")
    k, q = r % 2, r // 2
    n_chips = n_rows // 2
    here = swap_pairs(q)
    home = swap_pairs(c)
    distance = (here - home + n_chips) % n_chips
    step_on = 1 - 2 * k
    ring_to = swap_pairs((here + step_on + n_chips) % n_chips) * 2 + k
    ahead = jnp.where(k == 0, distance, (n_chips - distance) % n_chips)
    is_home = q == c
    sibling = r + 1 - 2 * k
    up = (r + n_rows - 1) % n_rows
    down = (r + 1) % n_rows
    left = (c + n_cols - 1) % n_cols
    right = (c + 1) % n_cols
    pending = []

    def put(cond, src, dst, send_sem, recv_sem, to):
        def make():
            return pltpu.make_async_remote_copy(
                src_ref=src, dst_ref=dst, send_sem=send_sem, recv_sem=recv_sem,
                device_id=to, device_id_type=MESH)

        @pl.when(cond)
        def _():
            make().start()

        pending.append((cond, make))

    def arrive(cond, dst, send_sem, recv_sem):
        @pl.when(cond)
        def _():
            pltpu.make_async_remote_copy(
                src_ref=dst, dst_ref=dst, send_sem=send_sem, recv_sem=recv_sem,
                device_id=(sibling, c), device_id_type=MESH).wait_recv()

    own = [pltpu.make_async_copy(cov.at[:, pl.ds(h * half, half)], pe.at[0, h, 1], local_sem.at[h]) for h in range(2)]
    own_dyn = pltpu.make_async_copy(dyn, drow.at[c], local_sem.at[2])
    own_fac = pltpu.make_async_copy(fac, nbuf.at[c], local_sem.at[3])
    for copy in (own_dyn, own_fac, own[0], own[1]):
        copy.start()

    barrier = pltpu.get_barrier_semaphore()
    for i in range(1, n_rows):
        pl.semaphore_signal(barrier, inc=1, device_id=((r + i) % n_rows, c), device_id_type=MESH)
    for i in range(1, n_cols):
        pl.semaphore_signal(barrier, inc=1, device_id=(r, (c + i) % n_cols), device_id_type=MESH)
    pl.semaphore_wait(barrier, n_rows + n_cols - 2)

    not_first, not_last = r > 0, r < n_rows - 1
    has_left, has_right = c > 0, c < n_cols - 1

    quarter = half // 2

    def columns(j):
        return pl.ds(j * quarter, quarter)

    detour = n_chips == 4
    upper, lower, last = n_rows // 2 - 1, n_rows // 2, n_rows - 1
    via_down, via_up = last, 0

    def send_half(step, h):
        for j in range(2):
            n = 2 * h + j
            src = cov.at[:, columns(n)] if step == 0 else pe.at[step, h, 1, :, columns(j)]
            goes_down, goes_up = not_last, not_first
            if detour and j == 1:
                goes_down = jnp.logical_and(not_last, r != upper)
                goes_up = jnp.logical_and(not_first, r != lower)
                block = rbuf.at[step, h]
                put(r == upper, src, block, rl_s.at[step, h], rl_r.at[step, h], (via_down, c))
                put(r == lower, src, block, rl_s.at[step, h], rl_r.at[step, h], (via_up, c))
            put(goes_down, src, pe.at[step, h, 0, :, columns(j)], pd_s.at[step, n], pd_r.at[step, n], (down, c))
            put(goes_up, src, pe.at[step, h, 2, :, columns(j)], pu_s.at[step, n], pu_r.at[step, n], (up, c))

    def relay_half(step, h):
        if not detour:
            return
        n, at, block = 2 * h + 1, columns(1), rbuf.at[step, h]
        arrive(jnp.logical_or(r == via_down, r == via_up), block, rl_s.at[step, h], rl_r.at[step, h])
        put(r == via_down, block, pe.at[step, h, 0, :, at], pd_s.at[step, n], pd_r.at[step, n], (lower, c))
        put(r == via_up, block, pe.at[step, h, 2, :, at], pu_s.at[step, n], pu_r.at[step, n], (upper, c))

    def to_plane(cond, z, i, src):
        go = jnp.logical_and(cond, is_home)
        put(go, src, dcol.at[k, z, i], rg_s.at[z, i], rg_r.at[z, i], (ring_to, c))
        put(go, src, dcol.at[k, z, i], sb_s.at[0, z, i], sb_r.at[k, z, i], (sibling, c))

    def ring_relay(cond, z, i, passes):
        block = dcol.at[k, z, i]
        arrive(cond, block, rg_s.at[z, i], rg_r.at[z, i])
        if passes:
            put(cond, block, block, rg_s.at[z, i], rg_r.at[z, i], (ring_to, c))
        put(cond, block, block, sb_s.at[1, z, i], sb_r.at[k, z, i], (sibling, c))

    for i in range(2):
        put(has_right, dyn.at[i], drow.at[c, i], zu_s.at[c, i], zu_r.at[c, i], (r, right))
        put(has_left, dyn.at[i], drow.at[c, i], zd_s.at[c, i], zd_r.at[c, i], (r, left))
    for i in range(2):
        to_plane(r >= 0, c, i, dyn.at[i])
    put(jnp.logical_not(is_home), fac, nbuf.at[c], nz_s, nz_r.at[c], (r, q))
    send_half(0, 0)
    send_half(0, 1)

    for step in range(STEPS):
        @pl.when(jnp.logical_not(not_first))
        def _():
            for h in range(2):
                pe[step, h, 0] = jnp.zeros((rows, half), F32)

        @pl.when(jnp.logical_not(not_last))
        def _():
            for h in range(2):
                pe[step, h, 2] = jnp.zeros((rows, half), F32)

        @pl.when(jnp.logical_not(has_left))
        def _():
            xe[step, 0] = jnp.zeros((rows, half), F32)

        @pl.when(jnp.logical_not(has_right))
        def _():
            xe[step, 3] = jnp.zeros((rows, half), F32)

    zero = jnp.zeros((band, band), BF16)
    for part in range(2):
        arow[part, 0, band:, :band] = zero
        arow[part, 2, :band, band:] = zero
        for j in range(2):
            acol[j, part, 0, band:, :band] = zero
            acol[j, part, 2, :band, band:] = zero
    noise[...] = jnp.zeros_like(noise)

    def sources(s):
        found = [(c - s >= 0, jnp.maximum(c - s, 0))]
        return found if s == 0 else found + [(c + s < n_cols, jnp.minimum(c + s, n_cols - 1))]

    def column_hop(s, i):
        (from_left, low), (from_right, high) = sources(s)
        block = drow.at[low, i]
        arrive(from_left, block, zu_s.at[low, i], zu_r.at[low, i])
        put(jnp.logical_and(from_left, has_right), block, block, zu_s.at[low, i], zu_r.at[low, i], (r, right))
        other = drow.at[high, i]
        arrive(from_right, other, zd_s.at[high, i], zd_r.at[high, i])
        put(jnp.logical_and(from_right, has_left), other, other, zd_s.at[high, i], zd_r.at[high, i], (r, left))
        to_plane(from_left, low, i, block)
        to_plane(from_right, high, i, other)

    def plane_hop(event, who, passes=True):
        for cond, z in sources(event // 2):
            ring_relay(jnp.logical_and(cond, who), z, event % 2, passes)

    n_events = 2 * n_cols
    leaf = ahead == n_chips - 1
    near = jnp.logical_and(ahead == 1, jnp.logical_not(leaf))
    far = jnp.logical_and(ahead > 1, jnp.logical_not(leaf))
    near_lag, far_lag = 5, 8
    for event in range(2, n_events):
        column_hop(event // 2, event % 2)
        if event in (n_events - 3, n_events - 1):
            relay_half(0, (event - n_events + 3) // 2)
        if event >= near_lag:
            plane_hop(event - near_lag, near)
        if event >= far_lag:
            plane_hop(event - far_lag, far)
    own_dyn.wait()

    def assemble(source, target):
        def block(i, o):
            return source[:, i, o].reshape(band, band)

        for i in range(2):
            for o in range(5):
                at = i + o
                hi, lo = split(block(i, o))
                span = pl.ds((at % 2) * band, band)
                target[0, at // 2, i * band:(i + 1) * band, span] = hi
                target[1, at // 2, i * band:(i + 1) * band, span] = lo

    assemble(drow, arow)
    own[0].wait()
    own[1].wait()

    def first_half(step, h):
        inner = product((arow[0, 1], arow[1, 1]), split(pe[step, h, 1]), False)
        for j in range(2):
            n, at = 2 * h + j, columns(j)
            if step > 0 and j == 1:
                relay_half(step, h)
            total = inner[:, j * quarter:(j + 1) * quarter]
            arrive(not_first, pe.at[step, h, 0, :, at], pd_s.at[step, n], pd_r.at[step, n])
            total += product((arow[0, 0], arow[1, 0]), split(pe[step, h, 0, :, at]), False)
            arrive(not_last, pe.at[step, h, 2, :, at], pu_s.at[step, n], pu_r.at[step, n])
            total += product((arow[0, 2], arow[1, 2]), split(pe[step, h, 2, :, at]), False)
            xe[step, 1 + h, :, at] = total
            src = xe.at[step, 1 + h, :, at]
            if h == 0:
                put(has_left, src, xe.at[step, 3, :, at], xl_s.at[step, j], xl_r.at[step, j], (r, left))
            else:
                put(has_right, src, xe.at[step, 0, :, at], xr_s.at[step, j], xr_r.at[step, j], (r, right))

    def second_half(step, h):
        def term(t):
            return product(split(xe[step, h + t]), (acol[h, 0, t], acol[h, 1, t]), True)

        if h == 0:
            total = term(1) + term(2) + noise[0]
            for j in range(2):
                arrive(has_left, xe.at[step, 0, :, columns(j)], xr_s.at[step, j], xr_r.at[step, j])
            total += term(0)
        else:
            total = term(0) + term(1) + noise[1]
            for j in range(2):
                arrive(has_right, xe.at[step, 3, :, columns(j)], xl_s.at[step, j], xl_r.at[step, j])
            total += term(2)
        if step + 1 < STEPS:
            pe[step + 1, h, 1] = total
            send_half(step + 1, h)
        else:
            obuf[h] = total
            pltpu.make_async_copy(obuf.at[h], out.at[:, pl.ds(h * half, half)], out_sem.at[h]).start()

    for event in range(n_events - near_lag, n_events):
        plane_hop(event, near)
    first_half(0, 0)
    for event in range(n_events - far_lag, n_events):
        plane_hop(event, far)
    first_half(0, 1)

    own_fac.wait()
    for z in range(n_cols):
        arrive(jnp.logical_and(is_home, c != z), nbuf.at[z], nz_s, nz_r.at[z])

    @pl.when(is_home)
    def _():
        for i in range(2):
            block = nbuf[:, i].reshape(band, band)
            block = 0.5 * (block + block.T)
            noise[k, i * band:(i + 1) * band, i * band:(i + 1) * band] = block

    for event in range(n_events):
        plane_hop(event, leaf, False)

    @pl.when(is_home)
    def _():
        acol[k] = arow[...]

    @pl.when(jnp.logical_not(is_home))
    def _():
        assemble(dcol.at[k], acol.at[k])

    for z in range(n_cols):
        for i in range(2):
            arrive(r >= 0, dcol.at[1 - k, z, i], sb_s.at[0, z, i], sb_r.at[1 - k, z, i])
    assemble(dcol.at[1 - k], acol.at[1 - k])

    def drain(sends):
        for cond, make in sends:
            @pl.when(cond)
            def _(make=make):
                make().wait_send()

    early = len(pending)
    for step in range(STEPS):
        order = (1, 0) if step % 2 == 0 else (0, 1)
        if step > 0:
            if step == 1:
                drain(pending[:early])
            for h in order[::-1]:
                first_half(step, h)
        for h in order:
            second_half(step, h)

    drain(pending[early:])
    for h in range(2):
        pltpu.make_async_copy(obuf.at[h], out.at[:, pl.ds(h * half, half)], out_sem.at[h]).wait()


def body(n_rows, n_cols, covariance, dynamics, noise_factor):
    rows, cols = covariance.shape
    band = dynamics.shape[3]
    half = cols // 2
    dma = pltpu.SemaphoreType.DMA
    shards = (n_cols, 2)
    pairs = (STEPS, 2)
    quarters = (STEPS, 4)
    return pl.pallas_call(
        functools.partial(kernel, n_rows, n_cols),
        out_shape=jax.ShapeDtypeStruct((rows, cols), F32),
        in_specs=[pl.BlockSpec(memory_space=pltpu.HBM)] * 3,
        out_specs=pl.BlockSpec(memory_space=pltpu.HBM),
        scratch_shapes=[
            pltpu.VMEM((STEPS, 2, 3, rows, half), F32),
            pltpu.VMEM((STEPS, 4, rows, half), F32),
            pltpu.VMEM((n_cols,) + dynamics.shape, F32),
            pltpu.VMEM((2, n_cols) + dynamics.shape, F32),
            pltpu.VMEM((n_cols,) + noise_factor.shape, F32),
            pltpu.VMEM((2, 3, rows, rows), BF16),
            pltpu.VMEM((2, 2, 3, rows, rows), BF16),
            pltpu.VMEM((2, rows, half), F32),
            pltpu.VMEM((2, rows, half), F32),
            pltpu.VMEM((STEPS, 2, rows, half // 2), F32),
            dma((4,)), dma((2,)),
            dma(shards), dma(shards), dma(shards), dma(shards),
            dma(shards), dma(shards), dma((2,) + shards), dma((2,) + shards),
            dma, dma((n_cols,)),
            dma(quarters), dma(quarters), dma(quarters), dma(quarters),
            dma(pairs), dma(pairs), dma(pairs), dma(pairs), dma(pairs), dma(pairs),
        ],
        compiler_params=pltpu.CompilerParams(
            collective_id=0, has_side_effects=True, vmem_limit_bytes=62 * 1024 * 1024),
    )(covariance, dynamics, noise_factor)


def solution(mesh):
    in_specs = (P("row", "col"), P("row", None, "col", None), P("row", "col", None))
    out_specs = P("row", "col")
    run = functools.partial(body, mesh.shape["row"], mesh.shape["col"])
    return jax.shard_map(run, mesh=mesh, in_specs=in_specs, out_specs=out_specs, check_vma=False)
```
